32 devices in a mesh: grp: 2 (over y), tp: 8 (over z, x), pd: 2 (over core).
Axes of the slice: x: 2, y: 2, z: 4, core: 2. Of those that a mesh axis runs over, the one named last changes fastest.
Arguments:
- prompt_hidden: bfloat16 [16, 2, 512, 5120], P(('grp', 'tp'), 'pd'), parts along dimension 0, may hold values from -7 to 8.5
- w_kv: bfloat16 [5120, 1024], P('tp'), may hold values from -0.09782797 to 0.09782797
- w_query: bfloat16 [5120, 2048], P('tp'), may hold values from -0.09782797 to 0.09782797
- w_out: bfloat16 [2048, 5120], P(None, 'tp'), may hold values from -0.125 to 0.125
- code_table: bfloat16 [39, 5120], P(None, 'tp'), may hold values from -2.4 to 2.8
- attn_gain: float32 [5120], P('tp'), may hold values from 0.5 to 1.5
- out_gain: float32 [5120], P('tp'), may hold values from 0.5 to 1.5
- head_weight: float32 [5120, 39], P('tp'), may hold values from -0.078125 to 0.078125
- decode_codes: int32 [16, 2, 4, 6], P('grp', 'pd'), parts along dimension 0, may hold values from 0 to 7, as said below
- page_owner: int32 [16, 2, 64, 1], P(('grp', 'tp'), 'pd'), parts along dimension 0, may hold values from 0 to 7; in each aligned block of 64 rows (0 to 63, 64 to 127, ..., all dimensions but the last counted through in order) at most 16 rows name the same one
- page_request: int32 [16, 2, 64], P(('grp', 'tp'), 'pd'), parts along dimension 0, may hold values from 0 to 3
- page_tokens: int32 [16, 2, 64], P(('grp', 'tp'), 'pd'), parts along dimension 0, may hold values from 1 to 8
Outputs:
- logits: float32 [16, 2, 4, 39], P(('grp', 'tp'), 'pd'), parts along dimension 0
The draws below stay inside these ranges and needn't reach their ends.
There are 2 independent parts, one for each index of `grp`. The reference program is written for one: setup_inputs(seed, part) draws one part's arguments, and reference() takes and returns one part's arrays. A program takes and returns all parts, laid end to end along the dimension named above; an argument that names none is the same for every part. Nothing has to cross between parts.
Inputs may be any that keep to these rules, and one draw needn't show every extreme that they name: `decode_codes`: code dimension d takes levels below its count (8, 8, 8, 5, 5, 5). `page_owner`: the pages of one device name one owner at most 16 times.
All inputs are finite; a program needn't handle non-finite values.
Results may differ from the reference program's by a relative error of at most 0.00105.
The reference program's roundings to bfloat16 on the way (of `cache`, `own`, `weights` and `attended`) count: a program that leaves them out, or rounds other values in their place, can miss the bound.
Values may be sent and summed in bfloat16 or wider, within the bound.
A program may use at most 64 MiB of HBM per device.

```python
import math
import jax
import jax.numpy as jnp
import numpy as np
from jax import lax

D = 5120
HD = 128
KVH = 4
QH = 16
CODES = 39
PAGE = 8
PTOK_DEV = 512
R_DEV = 4
PAGES_DEV = 64
CAP = 16
N_TP = 8
N_PD = 2


def draw_w_kv(key, part):
    key = jax.random.fold_in(key, 11)
    weights = jnp.clip(jax.random.normal(key, (D, 2 * KVH * HD), jnp.float32), -6.0, 6.0) * D ** (-0.5)
    return weights.astype(jnp.bfloat16)


def draw_w_query(key, part):
    key = jax.random.fold_in(key, 12)
    weights = jnp.clip(jax.random.normal(key, (D, QH * HD), jnp.float32), -6.0, 6.0) * D ** (-0.5)
    return weights.astype(jnp.bfloat16)


def draw_code_table(key, part):
    key = jax.random.fold_in(key, 13)
    table = jnp.clip(jax.random.normal(key, (CODES, D), jnp.float32), -6.0, 6.0) * 0.4
    return table.astype(jnp.bfloat16)


def draw_prompt_hidden(key, part):
    key = jax.random.fold_in(key, 17)
    noise_key = jax.random.fold_in(key, 0)
    states = jnp.clip(jax.random.normal(noise_key, (N_TP, N_PD, PTOK_DEV, D), jnp.float32), -6.0, 6.0)
    return states.astype(jnp.bfloat16)


def draw_decode_codes(key, part):
    key = jax.random.fold_in(key, 7)
    level_counts = jnp.array([8, 8, 8, 5, 5, 5], jnp.int32)
    return jax.random.randint(key, (N_TP, N_PD, R_DEV, 6), 0, level_counts, dtype=jnp.int32)


def touch_ends(drawn, rng, smallest, high):
    longest = drawn.shape.index(max(drawn.shape))
    spots = []
    for shift in (0, 1):
        where = [jax.random.randint(jax.random.fold_in(rng, axis), (), 0, length) for axis, length in enumerate(drawn.shape)]
        where[longest] = (where[longest] + shift) % drawn.shape[longest]
        spots.append(tuple(where))
    return drawn.at[spots[0]].set(smallest).at[spots[1]].set(high)


def block_levels(rng, dims, cuts, low, top_value):
    gain, own = 1.0, jax.random.fold_in(rng, 6)
    for axis_at, shards_of in cuts:
        heights = jnp.exp(jax.random.uniform(jax.random.fold_in(own, axis_at), (shards_of,), jnp.float32, low / len(cuts), top_value / len(cuts)))
        gain = gain * jnp.repeat(heights, dims[axis_at] // shards_of).reshape([-1 if axis == axis_at else 1 for axis in range(len(dims))])
    return gain


def shared_out(key, own, number, rows, number_of, top, most, skew):
    sequence = jax.random.permutation(key, number_of)
    packed, usual = load_shares(number_of, rows * top, most, skew, True), load_shares(number_of, rows * top, most, skew, False)
    places = jnp.arange(number_of)

    def named(lengths, rotation):
        used = int((lengths > 0).sum())
        fixed = max(1, used // 4)
        passed = fixed + (places - fixed + rotation * (used - fixed)) % max(1, number_of - fixed)
        return jnp.zeros((number_of,), jnp.int32).at[sequence[jnp.where(places < fixed, places, passed)]].set(jnp.asarray(lengths, jnp.int32))

    lengths = jnp.where(number % 4 == 0, named(packed, number // 4), named(usual, number - number // 4 - 1))
    mixed = jax.random.permutation(jax.random.fold_in(own, 3), number_of)
    source_of, sink = mixed[0:number_of // 2 * 2:2], mixed[1:number_of // 2 * 2:2]
    room = jnp.minimum(lengths[source_of] - 1, most - lengths[sink]) // 2
    room = jnp.where((source_of == sequence[0]) | (sink == sequence[0]) | (lengths[sink] == 0), 0, jnp.maximum(room, 0))
    passed = jax.random.randint(jax.random.fold_in(own, 4), (number_of // 2,), 0, 1 << 20) % (room + 1)
    lengths = lengths.at[source_of].add(-passed).at[sink].add(passed)
    members = jnp.searchsorted(jnp.cumsum(lengths), jnp.arange(rows * top), side="right").astype(jnp.int32)
    grid = members.reshape(top, rows).T
    grid = grid[jax.random.permutation(jax.random.fold_in(own, 1), rows)]
    rotation = jax.random.randint(jax.random.fold_in(own, 2), (rows, 1), 0, top)
    return jnp.take_along_axis(grid, (jnp.arange(top)[None, :] + rotation) % top, axis=1)


def load_shares(number_of, total, most, skew, full):
    portions = [(1 << 20) // math.isqrt(grade ** skew) + 1 for grade in range(1, number_of + 1)]
    largest = most if full else min(most, max(-(-total // number_of), total * portions[0] // sum(portions)))
    least = 1 if total - largest >= number_of - 1 else 0
    given, spare = [largest] + [least] * (number_of - 1), total - largest - least * (number_of - 1)
    while spare > 0:
        free = [i for i in range(1, number_of) if given[i] < largest] or [i for i in range(1, number_of) if given[i] < most]
        mass, remaining = sum([portions[i] for i in free]), spare
        for i in free:
            more = min(most - given[i], max(1, remaining * portions[i] // mass), spare)
            given[i] = given[i] + more
            spare = spare - more
    return np.array(given)


def gaussian(own_key, shape, spread, bound, cuts=(), kind=jnp.bfloat16):
    drawn = spread * jax.random.normal(own_key, shape, jnp.float32)
    if cuts:
        drawn = drawn * block_levels(own_key, shape, cuts, -0.22, 0.18)
    return jnp.clip(drawn, -bound, bound).astype(kind)


def setup_inputs(seed: int = 0, part: int = 0) -> dict:
    key_list = jax.random.split(jax.random.key(seed), 13)
    part_splits = jax.random.split(jax.random.fold_in(key_list[12], part), 13)
    prompt_hidden = draw_prompt_hidden(jax.random.fold_in(jax.random.fold_in(key_list[12], part), 71), part)
    w_kv = draw_w_kv(jax.random.fold_in(key_list[12], 71), part)
    w_query = draw_w_query(jax.random.fold_in(key_list[12], 71), part)
    w_out = gaussian(key_list[3], (QH * HD, D), (QH * HD) ** -0.5, 0.125, ((1, 8),))
    code_table = draw_code_table(jax.random.fold_in(key_list[12], 71), part)
    attn_gain = jnp.clip(1.0 + 0.1 * jax.random.normal(key_list[5], (D,), jnp.float32), 0.5, 1.5)
    out_gain = jnp.clip(1.0 + 0.1 * jax.random.normal(key_list[6], (D,), jnp.float32), 0.5, 1.5)
    head_weight = gaussian(key_list[7], (D, CODES), D ** -0.5, 0.078125, ((0, 8),), jnp.float32)
    decode_codes = draw_decode_codes(jax.random.fold_in(jax.random.fold_in(key_list[12], part), 71), part)
    page_owner_keys = jax.random.split(jax.random.fold_in(part_splits[9], 1), N_TP * N_PD * PAGES_DEV // PAGES_DEV)
    page_owner_turns = jax.random.permutation(jax.random.fold_in(part_splits[9], 3), N_TP * N_PD * PAGES_DEV // PAGES_DEV)
    page_owner = jax.vmap(lambda own, number: shared_out(jax.random.fold_in(part_splits[9], 2), own, number, PAGES_DEV, N_TP, 1, CAP, 2))(page_owner_keys, page_owner_turns).reshape((N_TP, N_PD, PAGES_DEV, 1))
    page_request = touch_ends(jax.random.randint(part_splits[10], (N_TP, N_PD, PAGES_DEV), 0, R_DEV), jax.random.fold_in(part_splits[10], 1), 0, R_DEV - 1).astype(jnp.int32)
    page_tokens = touch_ends(jax.random.randint(part_splits[11], (N_TP, N_PD, PAGES_DEV), 1, PAGE + 1), jax.random.fold_in(part_splits[11], 1), 1, PAGE).astype(jnp.int32)
    return {"prompt_hidden": prompt_hidden, "w_kv": w_kv, "w_query": w_query, "w_out": w_out, "code_table": code_table, "attn_gain": attn_gain, "out_gain": out_gain, "head_weight": head_weight, "decode_codes": decode_codes, "page_owner": page_owner, "page_request": page_request, "page_tokens": page_tokens}


fsq_levels = (8, 8, 8, 5, 5, 5)
eps = 1e-06

def code_hits(codes):
    columns = jnp.arange(CODES, dtype=jnp.int32)
    hits = jnp.zeros((codes.shape[0], CODES), jnp.float32)
    start = 0
    for dim_index in range(6):
        hits = hits + (codes[:, dim_index:dim_index + 1] + start == columns[None, :]).astype(jnp.float32)
        start = start + fsq_levels[dim_index]
    return hits

def attend(queries, new_keys, new_values, keys, values, live):
    scale = HD ** (-0.5)
    scores = jnp.einsum('rkgd,nkd->rkgn', queries.astype(jnp.float32), keys.astype(jnp.float32)) * scale
    own_score = jnp.einsum('rkgd,rkd->rkg', queries.astype(jnp.float32), new_keys.astype(jnp.float32)) * scale
    scores = jnp.where(live[:, None, None, :], scores, -jnp.inf)
    top = jnp.maximum(lax.optimization_barrier(jnp.max(scores, -1)), own_score)
    expo = jnp.exp(scores - top[..., None])
    own_expo = jnp.exp(own_score - top)
    total = lax.optimization_barrier(jnp.sum(expo, -1)) + own_expo
    weights = (expo / total[..., None]).astype(jnp.bfloat16)
    own_weight = (own_expo / total).astype(jnp.bfloat16)
    mixed = jnp.einsum('rkgn,nkd->rkgd', weights.astype(jnp.float32), values.astype(jnp.float32))
    mixed = mixed + own_weight.astype(jnp.float32)[..., None] * new_values.astype(jnp.float32)[:, :, None, :]
    return mixed.reshape(queries.shape[0], -1).astype(jnp.bfloat16)

def reference(prompt_hidden, w_kv, w_query, w_out, code_table, attn_gain, out_gain, head_weight, decode_codes, page_owner, page_request, page_tokens):
    kv_width = w_kv.shape[1]
    half = kv_width // 2
    query_width = w_query.shape[1]
    groups = QH // KVH
    owners = N_TP * N_PD
    blocks = prompt_hidden.reshape(N_TP * N_PD, PTOK_DEV, D)
    weight_kv = w_kv.astype(jnp.float32)

    def project_block(block):
        return jnp.dot(block.astype(jnp.float32), weight_kv, precision=lax.Precision.HIGHEST).astype(jnp.bfloat16)
    cache = lax.map(project_block, blocks).reshape(-1, kv_width)
    pages = cache.reshape(-1, PAGE, kv_width)
    pool = jnp.arange(N_PD, dtype=jnp.int32)[None, :, None]
    target = (page_owner[..., 0] * N_PD + (N_PD - 1 - pool)).reshape(-1).astype(jnp.int32)
    requests = page_request.reshape(-1)
    tokens = page_tokens.reshape(-1)
    order = jnp.argsort(target, stable=True)
    width_pages = N_TP * CAP
    sorted_pages = jnp.concatenate([pages[order], jnp.zeros((width_pages, PAGE, kv_width), jnp.bfloat16)], 0)
    sorted_requests = jnp.concatenate([requests[order], jnp.zeros((width_pages,), jnp.int32)], 0)
    sorted_tokens = jnp.concatenate([tokens[order], jnp.zeros((width_pages,), jnp.int32)], 0)
    counts = lax.optimization_barrier(jnp.sum((target[None, :] == jnp.arange(owners, dtype=jnp.int32)[:, None]).astype(jnp.int32), 1))
    starts = (jnp.cumsum(counts) - counts).astype(jnp.int32)
    codes = decode_codes.reshape(-1, 6)
    embedded = jnp.dot(code_hits(codes), code_table.astype(jnp.float32), precision=lax.Precision.HIGHEST)
    mean_square = lax.optimization_barrier(jnp.mean(embedded * embedded, 1, keepdims=True))
    normed = embedded * attn_gain[None, :] / jnp.sqrt(mean_square + eps)
    both = jnp.concatenate([w_query, w_kv], 1).astype(jnp.float32)
    own = jnp.dot(normed, both, precision=lax.Precision.HIGHEST).astype(jnp.bfloat16)

    def one_owner(owner):
        first = starts[owner]
        block = lax.dynamic_slice(sorted_pages, (first, jnp.int32(0), jnp.int32(0)), (width_pages, PAGE, kv_width))
        block_requests = lax.dynamic_slice(sorted_requests, (first,), (width_pages,))
        block_tokens = lax.dynamic_slice(sorted_tokens, (first,), (width_pages,))
        present = jnp.arange(width_pages, dtype=jnp.int32) < counts[owner]
        position = jnp.arange(PAGE, dtype=jnp.int32)
        token_live = (present[:, None] & (position[None, :] < block_tokens[:, None])).reshape(-1)
        token_request = jnp.broadcast_to(block_requests[:, None], (width_pages, PAGE)).reshape(-1)
        live = (token_request[None, :] == jnp.arange(R_DEV, dtype=jnp.int32)[:, None]) & token_live[None, :]
        store = block.reshape(width_pages * PAGE, 2, KVH, HD)
        rows = lax.dynamic_slice(own, (owner * R_DEV, jnp.int32(0)), (R_DEV, own.shape[1]))
        queries = rows[:, :query_width].reshape(R_DEV, KVH, groups, HD)
        new_keys = rows[:, query_width:query_width + half].reshape(R_DEV, KVH, HD)
        new_values = rows[:, query_width + half:].reshape(R_DEV, KVH, HD)
        return attend(queries, new_keys, new_values, store[:, 0], store[:, 1], live)
    attended = lax.map(one_owner, jnp.arange(owners, dtype=jnp.int32)).reshape(-1, query_width)
    branch = jnp.dot(attended.astype(jnp.float32), w_out.astype(jnp.float32), precision=lax.Precision.HIGHEST)
    hidden = embedded + branch
    mean_out = lax.optimization_barrier(jnp.mean(hidden * hidden, 1, keepdims=True))
    normed_out = hidden * out_gain[None, :] / jnp.sqrt(mean_out + eps)
    logits = jnp.dot(normed_out, head_weight, precision=lax.Precision.HIGHEST)
    return logits.reshape(N_TP, N_PD, R_DEV, CODES)
```

```python
import functools

import jax
import jax.numpy as jnp
from jax import lax
from jax.experimental import pallas as pl
from jax.experimental.pallas import tpu as pltpu
from jax.sharding import PartitionSpec as P

HD = 128
PAGE = 8
fsq_levels = (8, 8, 8, 5, 5, 5)
eps = 1e-06
LOW = -3e38
MESH = pl.DeviceIdType.MESH


def ring_index(k, n):
    late = k // (n // 2)
    return (1 - late) * (2 * k) + late * (2 * (n - 1 - k) + 1)


def kernel(
    n,
    per,
    prompt_ref,
    wkv_ref,
    wq_ref,
    wo_ref,
    table_ref,
    gain_ref,
    out_gain_ref,
    head_ref,
    codes_ref,
    label_ref,
    out_ref,
    pr,
    W,
    acc,
    kv,
    wq,
    wo,
    codes2,
    label2,
    emb,
    ownp,
    ownr,
    own_all,
    q_all,
    e_all,
    stat,
    statr,
    mixed,
    mixr,
    att,
    part,
    partr,
    loc,
    pd_send,
    pd_recv,
    p_send,
    p_recv,
    c_send,
    c_recv,
    y_send,
    y_recv,
    rs_send,
    rs_recv,
    ag_send,
    ag_recv,
    st_send,
    st_recv,
    mx_send,
    mx_recv,
    at_send,
    at_recv,
    lg_send,
    lg_recv,
):
    g = lax.axis_index("grp")
    me = lax.axis_index("tp")
    p = lax.axis_index("pd")
    rows = wkv_ref.shape[0]
    depth = prompt_ref.shape[1]
    toks = prompt_ref.shape[0]
    half = wkv_ref.shape[1] // 4
    qcols = wq_ref.shape[1] // 2
    cols = qcols + 2 * half
    heads = half // HD
    groups = qcols // half
    both = 2 * per
    R = n * both
    R4 = R * groups
    width = min(256, R4)
    chunks = R4 // width
    T = 2 * toks + R
    store = e_all is not None

    lo = pl.multiple_of(p * half, half)
    locals_ = [
        pltpu.make_async_copy(
            wkv_ref.at[:, pl.ds(lo, half)],
            W.at[pl.ds(pl.multiple_of(me * rows, 16), rows), pl.ds(0, half)],
            loc.at[0],
        ),
        pltpu.make_async_copy(
            wkv_ref.at[:, pl.ds(pl.multiple_of(2 * half + p * half, half), half)],
            W.at[pl.ds(pl.multiple_of(me * rows, 16), rows), pl.ds(half, half)],
            loc.at[1],
        ),
        pltpu.make_async_copy(
            wq_ref.at[:, pl.ds(pl.multiple_of(p * qcols, qcols), qcols)], wq, loc.at[2]
        ),
        pltpu.make_async_copy(prompt_ref, pr.at[pl.ds(0, toks)], loc.at[3]),
        pltpu.make_async_copy(wo_ref, wo, loc.at[4]),
    ]
    for copy in locals_:
        copy.start()

    barrier = pltpu.get_barrier_semaphore()

    @pl.loop(1, n)
    def _(i):
        j = (me + i) % n
        pl.semaphore_signal(barrier, inc=1, device_id={"tp": j}, device_id_type=MESH)
        pl.semaphore_signal(
            barrier, inc=1, device_id={"tp": j, "pd": 1 - p}, device_id_type=MESH
        )

    pl.semaphore_signal(barrier, inc=1, device_id={"pd": 1 - p}, device_id_type=MESH)
    pl.semaphore_signal(barrier, inc=1, device_id={"grp": 1 - g}, device_id_type=MESH)
    pl.semaphore_wait(barrier, 2 * n)

    def remote(src, dst, send, recv, **where):
        return pltpu.make_async_remote_copy(
            src_ref=src,
            dst_ref=dst,
            send_sem=send,
            recv_sem=recv,
            device_id=where,
            device_id_type=MESH,
        )

    crossed = [
        remote(codes_ref, codes2, pd_send.at[0], pd_recv.at[0], pd=1 - p),
        remote(label_ref, label2, pd_send.at[1], pd_recv.at[1], pd=1 - p),
        remote(prompt_ref, pr.at[pl.ds(toks, toks)], pd_send.at[2], pd_recv.at[2], pd=1 - p),
    ]
    for copy in crossed:
        copy.start()

    share = rows // 16 // 3 * 16
    rest = rows - 2 * share
    pos = (1 - me % 2) * (me // 2) + (me % 2) * (n - 1 - me // 2)
    right = ring_index((pos + 1) % n, n)
    left = ring_index((pos + n - 1) % n, n)

    def p_rows(s, twin):
        o = ring_index((pos + n - s) % n, n)
        at = o * rows + ((1 - g) if twin else g) * share
        return W.at[pl.ds(pl.multiple_of(at, 16), share)]

    def c_rows(s):
        o = ring_index((pos + s) % n, n)
        return W.at[pl.ds(pl.multiple_of(o * rows + 2 * share, 16), rest)]

    def p_copy(s):
        return remote(p_rows(s, False), p_rows(s, False), p_send.at[s], p_recv.at[s + 1], tp=right)

    def c_copy(s):
        return remote(c_rows(s), c_rows(s), c_send.at[s], c_recv.at[s + 1], tp=left)

    def y_copy(s):
        return remote(p_rows(s, False), p_rows(s, False), y_send.at[s], y_recv.at[s], grp=1 - g)

    def p_wait(s):
        remote(p_rows(s, False), p_rows(s, False), p_send.at[s], p_recv.at[s], tp=right).wait_recv()

    def c_wait(s):
        remote(c_rows(s), c_rows(s), c_send.at[s], c_recv.at[s], tp=left).wait_recv()

    def y_wait(s):
        remote(p_rows(s, True), p_rows(s, True), y_send.at[s], y_recv.at[s], grp=1 - g).wait_recv()

    def step(s, last=False):
        p_wait(s)
        if not last:
            p_copy(s).start()
        y_copy(s).start()
        c_wait(s)
        if not last:
            c_copy(s).start()

    aligned = rows % 128 == 0
    strip = 256

    def multiply(o, first):
        if not aligned:
            return

        @pl.loop(0, 2 * toks // strip)
        def _(b):
            at = pl.ds(pl.multiple_of(b * strip, strip), strip)
            term = jnp.dot(
                pr[at, pl.ds(pl.multiple_of(o * rows, 128), rows)],
                W[pl.ds(pl.multiple_of(o * rows, 16), rows), :],
                preferred_element_type=jnp.float32,
            )
            if first:
                acc[at, :] = term
            else:
                acc[at, :] += term

    locals_[0].wait()
    locals_[1].wait()
    p_copy(0).start()
    c_copy(0).start()

    crossed[0].wait()
    codes = codes_ref[...] + codes2[...]
    levels = table_ref.shape[0]
    columns = lax.broadcasted_iota(jnp.int32, (R, levels), 1) + 1
    hits = jnp.zeros((R, levels), jnp.float32)
    for d in range(6):
        hits = hits + jnp.where(codes[:, d : d + 1] == columns, 1.0, 0.0)
    embedded = jnp.dot(
        hits.astype(jnp.bfloat16), table_ref[...], preferred_element_type=jnp.float32
    )
    emb[...] = embedded
    ownp[:, cols:] = jnp.broadcast_to(jnp.sum(embedded * embedded, 1, keepdims=True), (R, 128))
    x = embedded * gain_ref[...]
    x1 = x.astype(jnp.bfloat16)
    x = x - x1.astype(jnp.float32)
    x2 = x.astype(jnp.bfloat16)
    x3 = (x - x2.astype(jnp.float32)).astype(jnp.bfloat16)
    xs = jnp.concatenate([x1, x2, x3], 0)

    def summed(y):
        return y[:R] + y[R : 2 * R] + y[2 * R :]

    ownp[:, qcols:cols] = summed(
        jnp.dot(
            xs,
            W[pl.ds(pl.multiple_of(me * rows, 16), rows), :],
            preferred_element_type=jnp.float32,
        )
    )
    locals_[2].wait()
    ownp[:, :qcols] = summed(jnp.dot(xs, wq[...], preferred_element_type=jnp.float32))

    def block(ref, j):
        return ref.at[pl.ds(pl.multiple_of(j * both, both), both)]

    def scatter(src, dst, send, recv):
        def copy(i):
            j = (me + i) % n
            return remote(block(src, j), dst.at[i], send.at[i], recv.at[i], tp=j)

        return copy

    def every(copy, act):
        @pl.loop(1, n)
        def _(i):
            act(copy(i))

    def go(copy):
        copy.start()

    def got(copy):
        copy.wait_recv()

    def sent(copy):
        copy.wait_send()

    def total(src, dst):
        def add(i, running):
            return running + dst[i]

        return lax.fori_loop(1, n, add, src[pl.ds(pl.multiple_of(me * both, both), both), :])

    rs = scatter(ownp, ownr, rs_send, rs_recv)
    every(rs, go)

    mid = n // 2

    @pl.loop(1, mid - 1)
    def _(s):
        step(s)

    every(rs, got)
    whole = total(ownp, ownr)
    own = whole[:, :cols] * lax.rsqrt(whole[:, cols : cols + 1] / depth + eps)
    own_all[pl.ds(pl.multiple_of(me * both, both), both), :] = own.astype(jnp.bfloat16).astype(
        jnp.float32
    )

    def ag(i):
        j = (me + i) % n
        return remote(
            block(own_all, me), block(own_all, me), ag_send.at[i], ag_recv.at[i], tp=j
        )

    def ag_wait(i):
        j = (me + n - i) % n
        remote(
            block(own_all, j), block(own_all, j), ag_send.at[i], ag_recv.at[i], tp=j
        ).wait_recv()

    every(ag, go)
    step(mid - 1)
    locals_[3].wait()
    crossed[2].wait()
    multiply(me, True)
    step(mid)
    y_wait(mid)
    multiply(ring_index((pos + mid) % n, n), False)

    def late(s, last):
        step(s, last)
        y_wait(n - s)
        multiply(ring_index((pos + s) % n, n), False)
        y_wait(s)
        multiply(ring_index((pos + n - s) % n, n), False)

    @pl.loop(mid + 1, n - 1)
    def _(s):
        late(s, False)

    pl.loop(1, n)(ag_wait)
    crossed[1].wait()
    for k in range(heads):
        for c in range(groups):
            at = (k * groups + c) * HD
            q_all[k, c * R : (c + 1) * R, :] = own_all[:, at : at + HD].astype(jnp.bfloat16)
    kv[2 * toks :, :] = own_all[:, qcols:].astype(jnp.bfloat16)
    late(n - 1, True)

    @pl.loop(0, 2 * toks // strip)
    def _(b):
        at = pl.ds(pl.multiple_of(b * strip, strip), strip)
        if aligned:
            kv[at, :] = acc[at, :].astype(jnp.bfloat16)
        else:
            kv[at, :] = jnp.dot(
                pr[at, :], W[...], preferred_element_type=jnp.float32
            ).astype(jnp.bfloat16)

    scale = HD ** (-0.5)
    mine = lax.broadcasted_iota(jnp.int32, (R, 1), 0)
    mine = jnp.where(mine // both == me, mine, -1)
    label = jnp.concatenate([label_ref[:, :1], label2[:, :1], mine], 0)

    def scored(k, c):
        row = (lax.broadcasted_iota(jnp.int32, (T, width), 1) + c * width) % R
        live = label == row
        s = lax.dot_general(
            kv[:, k * HD : (k + 1) * HD],
            q_all[k, c * width : (c + 1) * width, :],
            (((1,), (1,)), ((), ())),
            preferred_element_type=jnp.float32,
        )
        s = jnp.where(live, s * scale, LOW)
        m = jnp.max(s, 0, keepdims=True)
        return jnp.where(live, jnp.exp(s - m), 0.0), m

    for k in range(heads):
        for c in range(chunks):
            at = slice(c * width, (c + 1) * width)
            e, m = scored(k, c)
            if store:
                e_all[k * chunks + c] = e
            stat[k : k + 1, at] = m
            stat[heads + k : heads + k + 1, at] = jnp.sum(e, 0, keepdims=True)

    def st(i):
        return remote(stat, statr.at[i], st_send.at[i], st_recv.at[i], tp=(me + i) % n)

    every(st, go)
    every(st, got)
    statr[0] = stat[...]

    def top_of(i, running):
        return jnp.maximum(running, statr[i, :heads, :])

    top = lax.fori_loop(1, n, top_of, stat[:heads, :])

    def sum_of(i, running):
        return running + statr[i, heads : 2 * heads, :] * jnp.exp(statr[i, :heads, :] - top)

    sums = lax.fori_loop(0, n, sum_of, jnp.zeros_like(top))
    factor = jnp.exp(stat[:heads, :] - top) / sums

    for k in range(heads):
        for c in range(chunks):
            e = e_all[k * chunks + c] if store else scored(k, c)[0]
            weights = (e * factor[k : k + 1, c * width : (c + 1) * width]).astype(jnp.bfloat16)
            out = lax.dot_general(
                weights,
                kv[:, half + k * HD : half + (k + 1) * HD],
                (((0,), (0,)), ((), ())),
                preferred_element_type=jnp.float32,
            )
            size = min(width, R)
            for piece in range(width // size):
                head, first = divmod(c * width + piece * size, R)
                at = (k * groups + head) * HD
                mixed[first : first + size, at : at + HD] = out[
                    piece * size : (piece + 1) * size
                ]

    mx = scatter(mixed, mixr, mx_send, mx_recv)
    every(mx, go)
    every(mx, got)
    attended = total(mixed, mixr)
    att[p, me] = jnp.concatenate([attended[:, : qcols // 2], attended[:, qcols // 2 :]], 0).astype(
        jnp.bfloat16
    )

    def at_copy(c):
        def copy(i):
            q = (p + c) % 2
            return remote(
                att.at[p, me], att.at[p, me], at_send.at[c, i], at_recv.at[c, i], tp=(me + i) % n, pd=q
            )

        return copy

    def at_wait(c):
        def wait(i):
            q = (p + c) % 2
            j = (me + n - i) % n
            remote(
                att.at[q, j], att.at[q, j], at_send.at[c, i], at_recv.at[c, i], tp=j, pd=q
            ).wait_recv()

        return wait

    pl.loop(1, n)(lambda i: go(at_copy(0)(i)))
    pl.loop(0, n)(lambda i: go(at_copy(1)(i)))
    locals_[4].wait()
    pl.loop(1, n)(at_wait(0))
    pl.loop(0, n)(at_wait(1))

    hidden = emb[...]
    for q in range(2):
        got_att = att[q].astype(jnp.float32)
        for h in range(2):
            lhs = got_att[:, h * both : (h + 1) * both, :].reshape(R, qcols // 2)
            at = q * qcols + h * (qcols // 2)
            hidden = hidden + jnp.dot(
                lhs.astype(jnp.bfloat16),
                wo[at : at + qcols // 2, :],
                preferred_element_type=jnp.float32,
            )
    part[...] = jnp.broadcast_to(jnp.sum(hidden * hidden, 1, keepdims=True), (R, 128))
    part[:, :levels] = jnp.dot(
        hidden * out_gain_ref[...],
        head_ref[...],
        precision=lax.Precision.HIGHEST,
        preferred_element_type=jnp.float32,
    )
    lg = scatter(part, partr, lg_send, lg_recv)
    every(lg, go)
    every(lg, got)
    final = total(part, partr)
    final = final[:, :levels] * lax.rsqrt(final[:, 127:128] / depth + eps)
    out_ref[...] = jnp.where(p == 0, final[:per], final[per:])

    for copy in (rs, ag, st, mx, lg, at_copy(0)):
        every(copy, sent)
    pl.loop(0, n)(lambda i: sent(at_copy(1)(i)))

    @pl.loop(0, n - 1)
    def _(s):
        p_copy(s).wait_send()
        c_copy(s).wait_send()

    @pl.loop(1, n)
    def _(s):
        y_copy(s).wait_send()


def body(
    prompt_hidden,
    w_kv,
    w_query,
    w_out,
    code_table,
    attn_gain,
    out_gain,
    head_weight,
    decode_codes,
    page_owner,
    page_request,
    page_tokens,
):
    n = lax.axis_size("tp")
    p = lax.axis_index("pd")
    toks, depth = prompt_hidden.shape[2:]
    per = decode_codes.shape[2]
    both = 2 * per
    R = n * both
    rows, kv_width = w_kv.shape
    half = kv_width // 4
    qcols = w_query.shape[1] // 2
    cols = qcols + 2 * half
    heads = half // HD
    groups = qcols // half
    R4 = R * groups
    width = min(256, R4)
    T = 2 * toks + R
    starts = jnp.array([1 + sum(fsq_levels[:d]) for d in range(6)], jnp.int32)
    codes = decode_codes[:, 0] + starts
    slot = lax.broadcasted_iota(jnp.int32, (n, 2, per, 6), 1)
    codes = jnp.where(slot == p, codes[:, None], 0).reshape(R, 6)
    codes = jnp.pad(codes, ((0, 0), (0, 122)))
    target = page_owner.reshape(-1) * both + (1 - p) * per + page_request.reshape(-1)
    position = jnp.arange(PAGE, dtype=jnp.int32)
    label = jnp.where(
        position[None, :] < page_tokens.reshape(-1)[:, None], target[:, None], -1
    )
    label = jnp.broadcast_to(label[:, :, None], label.shape + (128,)).reshape(toks, 128)

    bf, f32 = jnp.bfloat16, jnp.float32
    store = heads * T * R4 * 4 <= 8 << 20
    dma = pltpu.SemaphoreType.DMA
    hbm = pl.BlockSpec(memory_space=pl.ANY)
    vmem = pl.BlockSpec(memory_space=pltpu.VMEM)
    scratch = [
        pltpu.VMEM((2 * toks, depth), bf),
        pltpu.VMEM((depth, 2 * half), bf),
        pltpu.VMEM((2 * toks, 2 * half), f32),
        pltpu.VMEM((T, 2 * half), bf),
        pltpu.VMEM((rows, qcols), bf),
        pltpu.VMEM(w_out.shape, bf),
        pltpu.VMEM((R, 128), jnp.int32),
        pltpu.VMEM((toks, 128), jnp.int32),
        pltpu.VMEM((R, rows), f32),
        pltpu.VMEM((R, cols + 128), f32),
        pltpu.VMEM((n, both, cols + 128), f32),
        pltpu.VMEM((R, cols), f32),
        pltpu.VMEM((heads, R4, HD), bf),
        pltpu.VMEM((heads * R4 // width, T, width), f32) if store else None,
        pltpu.VMEM((8, R4), f32),
        pltpu.VMEM((n, 8, R4), f32),
        pltpu.VMEM((R, qcols), f32),
        pltpu.VMEM((n, both, qcols), f32),
        pltpu.VMEM((2, n, 2 * both, qcols // 2), bf),
        pltpu.VMEM((R, 128), f32),
        pltpu.VMEM((n, both, 128), f32),
        dma((5,)),
        dma((3,)),
        dma((3,)),
    ] + [dma((n,))] * 14 + [dma((2, n))] * 2 + [dma((n,))] * 2
    run = functools.partial(kernel, n, per)
    if not store:
        at = 11 + 13
        scratch.pop(13)
        full = run

        def run(*refs):
            return full(*refs[:at], None, *refs[at:])

    logits = pl.pallas_call(
        run,
        out_shape=jax.ShapeDtypeStruct((per, head_weight.shape[1]), f32),
        in_specs=[hbm, hbm, hbm, hbm, vmem, vmem, vmem, vmem, vmem, vmem],
        out_specs=vmem,
        scratch_shapes=scratch,
        compiler_params=pltpu.CompilerParams(
            collective_id=0, has_side_effects=True, vmem_limit_bytes=60 << 20
        ),
    )(
        prompt_hidden.reshape(toks, depth),
        w_kv,
        w_query,
        w_out,
        code_table,
        attn_gain.reshape(1, rows),
        out_gain.reshape(1, rows),
        head_weight,
        codes,
        label,
    )
    return logits.reshape(1, 1, per, -1)


def solution(mesh):
    return jax.shard_map(
        body,
        mesh=mesh,
        in_specs=(
            P(("grp", "tp"), "pd", None, None),
            P("tp", None),
            P("tp", None),
            P(None, "tp"),
            P(None, "tp"),
            P("tp"),
            P("tp"),
            P("tp", None),
            P("grp", "pd", None, None),
            P(("grp", "tp"), "pd", None, None),
            P(("grp", "tp"), "pd", None),
            P(("grp", "tp"), "pd", None),
        ),
        out_specs=P(("grp", "tp"), "pd", None, None),
        check_vma=False,
    )
```

```python
import functools

import jax
import jax.numpy as jnp
from jax import lax
from jax.experimental import pallas as pl
from jax.experimental.pallas import tpu as pltpu
from jax.sharding import PartitionSpec as P

HD = 128
PAGE = 8
fsq_levels = (8, 8, 8, 5, 5, 5)
eps = 1e-06
LOW = -3e38
PIECES = 3
MESH = pl.DeviceIdType.MESH


def ring_index(k, n):
    late = k // (n // 2)
    return (1 - late) * (2 * k) + late * (2 * (n - 1 - k) + 1)


def pieces(rows):
    units = rows // 16
    count = min(PIECES, units)
    cuts = [units * i // count * 16 for i in range(count + 1)]
    return [(low, high - low) for low, high in zip(cuts, cuts[1:])]


def kernel(
    n,
    per,
    prompt_ref,
    wkv_ref,
    wq_ref,
    wo_ref,
    table_ref,
    gain_ref,
    out_gain_ref,
    head_ref,
    meta_ref,
    out_ref,
    pr,
    W,
    acc,
    kv,
    wq,
    wo,
    meta2,
    emb,
    ownp,
    ownr,
    own_all,
    q_all,
    e_all,
    stat,
    statr,
    mixed,
    mixr,
    att,
    part,
    partr,
    loc,
    pd_send,
    pd_recv,
    p_send,
    p_recv,
    c_send,
    c_recv,
    y_send,
    y_recv,
    rs_send,
    rs_recv,
    ag_send,
    ag_recv,
    st_send,
    st_recv,
    mx_send,
    mx_recv,
    at_send,
    at_recv,
    lg_send,
    lg_recv,
):
    g = lax.axis_index("grp")
    me = lax.axis_index("tp")
    p = lax.axis_index("pd")
    rows = wkv_ref.shape[0]
    depth = prompt_ref.shape[1]
    toks = prompt_ref.shape[0]
    half = wkv_ref.shape[1] // 4
    qcols = wq_ref.shape[1] // 2
    cols = qcols + 2 * half
    heads = half // HD
    groups = qcols // half
    both = 2 * per
    R = n * both
    R4 = R * groups
    width = min(256, R4)
    chunks = R4 // width
    T = 2 * toks + R
    store = e_all is not None

    lo = pl.multiple_of(p * half, half)
    locals_ = [
        pltpu.make_async_copy(
            wkv_ref.at[:, pl.ds(lo, half)],
            W.at[pl.ds(pl.multiple_of(me * rows, 16), rows), pl.ds(0, half)],
            loc.at[0],
        ),
        pltpu.make_async_copy(
            wkv_ref.at[:, pl.ds(pl.multiple_of(2 * half + p * half, half), half)],
            W.at[pl.ds(pl.multiple_of(me * rows, 16), rows), pl.ds(half, half)],
            loc.at[1],
        ),
        pltpu.make_async_copy(
            wq_ref.at[:, pl.ds(pl.multiple_of(p * qcols, qcols), qcols)], wq, loc.at[2]
        ),
        pltpu.make_async_copy(prompt_ref, pr.at[pl.ds(0, toks)], loc.at[3]),
        pltpu.make_async_copy(wo_ref, wo, loc.at[4]),
    ]
    for copy in locals_:
        copy.start()

    barrier = pltpu.get_barrier_semaphore()

    @pl.loop(1, n)
    def _(i):
        j = (me + i) % n
        pl.semaphore_signal(barrier, inc=1, device_id={"tp": j}, device_id_type=MESH)
        pl.semaphore_signal(
            barrier, inc=1, device_id={"tp": j, "pd": 1 - p}, device_id_type=MESH
        )

    pl.semaphore_signal(barrier, inc=1, device_id={"pd": 1 - p}, device_id_type=MESH)
    pl.semaphore_signal(barrier, inc=1, device_id={"grp": 1 - g}, device_id_type=MESH)
    pl.semaphore_wait(barrier, 2 * n)

    def remote(src, dst, send, recv, **where):
        return pltpu.make_async_remote_copy(
            src_ref=src,
            dst_ref=dst,
            send_sem=send,
            recv_sem=recv,
            device_id=where,
            device_id_type=MESH,
        )

    crossed = [
        remote(meta_ref, meta2, pd_send.at[0], pd_recv.at[0], pd=1 - p),
        remote(prompt_ref, pr.at[pl.ds(toks, toks)], pd_send.at[1], pd_recv.at[1], pd=1 - p),
    ]
    for copy in crossed:
        copy.start()

    share = rows // 16 // 3 * 16
    rest = rows - 2 * share
    p_parts, c_parts = pieces(share), pieces(rest)
    pos = (1 - me % 2) * (me // 2) + (me % 2) * (n - 1 - me // 2)
    right = ring_index((pos + 1) % n, n)
    left = ring_index((pos + n - 1) % n, n)

    def p_rows(s, h, twin):
        o = ring_index((pos + n - s) % n, n)
        first, size = p_parts[h]
        at = o * rows + ((1 - g) if twin else g) * share + first
        return W.at[pl.ds(pl.multiple_of(at, 16), size)]

    def c_rows(s, h):
        o = ring_index((pos + s) % n, n)
        first, size = c_parts[h]
        return W.at[pl.ds(pl.multiple_of(o * rows + 2 * share + first, 16), size)]

    def p_copy(s, h):
        ref = p_rows(s, h, False)
        return remote(ref, ref, p_send.at[h, s], p_recv.at[h, s + 1], tp=right)

    def c_copy(s, h):
        ref = c_rows(s, h)
        return remote(ref, ref, c_send.at[h, s], c_recv.at[h, s + 1], tp=left)

    def y_copy(s, h):
        ref = p_rows(s, h, False)
        return remote(ref, ref, y_send.at[h, s], y_recv.at[h, s], grp=1 - g)

    def y_wait(s):
        for h in range(len(p_parts)):
            ref = p_rows(s, h, True)
            remote(ref, ref, y_send.at[h, s], y_recv.at[h, s], grp=1 - g).wait_recv()

    def step(s, last=False):
        for h in range(len(c_parts)):
            if h < len(p_parts):
                ref = p_rows(s, h, False)
                remote(ref, ref, p_send.at[h, s], p_recv.at[h, s], tp=right).wait_recv()
                if not last:
                    p_copy(s, h).start()
                y_copy(s, h).start()
            ref = c_rows(s, h)
            remote(ref, ref, c_send.at[h, s], c_recv.at[h, s], tp=left).wait_recv()
            if not last:
                c_copy(s, h).start()

    mid = n // 2
    aligned = rows % 128 == 0
    strip = 256

    def multiply(o, first):
        if not aligned:
            return

        @pl.loop(0, 2 * toks // strip)
        def _(b):
            at = pl.ds(pl.multiple_of(b * strip, strip), strip)
            term = jnp.dot(
                pr[at, pl.ds(pl.multiple_of(o * rows, 128), rows)],
                W[pl.ds(pl.multiple_of(o * rows, 16), rows), :],
                preferred_element_type=jnp.float32,
            )
            if first:
                acc[at, :] = term
            else:
                acc[at, :] += term

    locals_[0].wait()
    locals_[1].wait()
    for h in range(len(c_parts)):
        if h < len(p_parts):
            p_copy(0, h).start()
        c_copy(0, h).start()

    crossed[0].wait()
    ours, theirs = meta_ref[...].astype(jnp.float32), meta2[...].astype(jnp.float32)
    lanes = meta_ref.shape[1]
    row = lax.broadcasted_iota(jnp.int32, (R, lanes), 0)
    chosen = lax.broadcasted_iota(jnp.int32, (R, lanes), 1) == row % per * n + row // both
    from_ours = row // per % 2 == p
    levels = table_ref.shape[0]
    columns = lax.broadcasted_iota(jnp.int32, (R, levels), 1).astype(jnp.float32)
    hits = jnp.zeros((R, levels), jnp.float32)
    for d in range(6):
        codes = jnp.where(from_ours, ours[d : d + 1], theirs[d : d + 1])
        codes = jnp.sum(jnp.where(chosen, codes, 0.0), 1, keepdims=True)
        hits = hits + jnp.where(codes == columns, 1.0, 0.0)
    embedded = jnp.dot(
        hits.astype(jnp.bfloat16), table_ref[...], preferred_element_type=jnp.float32
    )
    emb[...] = embedded
    ownp[:, cols:] = jnp.broadcast_to(jnp.sum(embedded * embedded, 1, keepdims=True), (R, 128))
    x = embedded * gain_ref[...].reshape(1, rows)
    x1 = x.astype(jnp.bfloat16)
    x = x - x1.astype(jnp.float32)
    x2 = x.astype(jnp.bfloat16)
    x3 = (x - x2.astype(jnp.float32)).astype(jnp.bfloat16)
    xs = jnp.concatenate([x1, x2, x3], 0)

    def summed(y):
        return y[:R] + y[R : 2 * R] + y[2 * R :]

    ownp[:, qcols:cols] = summed(
        jnp.dot(
            xs,
            W[pl.ds(pl.multiple_of(me * rows, 16), rows), :],
            preferred_element_type=jnp.float32,
        )
    )
    if mid > 2:
        step(1)
    locals_[2].wait()
    ownp[:, :qcols] = summed(jnp.dot(xs, wq[...], preferred_element_type=jnp.float32))

    def block(ref, j):
        return ref.at[pl.ds(pl.multiple_of(j * both, both), both)]

    def scatter(src, dst, send, recv):
        def copy(i):
            j = (me + i) % n
            return remote(block(src, j), dst.at[i], send.at[i], recv.at[i], tp=j)

        return copy

    def every(copy, act):
        @pl.loop(1, n)
        def _(i):
            act(copy(i))

    def go(copy):
        copy.start()

    def got(copy):
        copy.wait_recv()

    def sent(copy):
        copy.wait_send()

    def total(src, dst):
        def add(i, running):
            return running + dst[i]

        return lax.fori_loop(1, n, add, src[pl.ds(pl.multiple_of(me * both, both), both), :])

    rs = scatter(ownp, ownr, rs_send, rs_recv)
    every(rs, go)

    @pl.loop(2, mid - 1)
    def _(s):
        step(s)

    step(mid - 1)
    locals_[3].wait()
    crossed[1].wait()
    multiply(me, True)
    step(mid)
    y_wait(mid)
    multiply(ring_index((pos + mid) % n, n), False)

    every(rs, got)
    whole = total(ownp, ownr)
    own = whole[:, :cols] * lax.rsqrt(whole[:, cols : cols + 1] / depth + eps)
    own_all[pl.ds(pl.multiple_of(me * both, both), both), :] = own.astype(jnp.bfloat16).astype(
        jnp.float32
    )

    def ag(i):
        j = (me + i) % n
        return remote(
            block(own_all, me), block(own_all, me), ag_send.at[i], ag_recv.at[i], tp=j
        )

    def ag_wait(i):
        j = (me + n - i) % n
        remote(
            block(own_all, j), block(own_all, j), ag_send.at[i], ag_recv.at[i], tp=j
        ).wait_recv()

    every(ag, go)

    def late(s, last):
        step(s, last)
        y_wait(n - s)
        multiply(ring_index((pos + s) % n, n), False)
        y_wait(s)
        multiply(ring_index((pos + n - s) % n, n), False)

    @pl.loop(mid + 1, n - 1)
    def _(s):
        late(s, False)

    pl.loop(1, n)(ag_wait)
    for k in range(heads):
        for c in range(groups):
            at = (k * groups + c) * HD
            q_all[k, c * R : (c + 1) * R, :] = own_all[:, at : at + HD].astype(jnp.bfloat16)
    kv[2 * toks :, :] = own_all[:, qcols:].astype(jnp.bfloat16)
    late(n - 1, True)

    @pl.loop(0, 2 * toks // strip)
    def _(b):
        at = pl.ds(pl.multiple_of(b * strip, strip), strip)
        if aligned:
            kv[at, :] = acc[at, :].astype(jnp.bfloat16)
        else:
            kv[at, :] = jnp.dot(
                pr[at, :], W[...], preferred_element_type=jnp.float32
            ).astype(jnp.bfloat16)

    scale = HD ** (-0.5)
    mine = lax.broadcasted_iota(jnp.int32, (R, 1), 0)
    mine = jnp.where(mine // both == me, mine, -1)
    token = lax.broadcasted_iota(jnp.int32, (toks, lanes), 0)
    in_page = token // PAGE == lax.broadcasted_iota(jnp.int32, (toks, lanes), 1)
    position = lax.broadcasted_iota(jnp.int32, (toks, 1), 0) % PAGE

    def labels(rows_of):
        target, filled = [
            jnp.sum(jnp.where(in_page, rows_of[i : i + 1], 0.0), 1, keepdims=True).astype(jnp.int32)
            for i in (6, 7)
        ]
        return jnp.where(position < filled, target, -1)

    label = jnp.concatenate([labels(ours), labels(theirs), mine], 0)

    def scored(k, c):
        row = (lax.broadcasted_iota(jnp.int32, (T, width), 1) + c * width) % R
        live = label == row
        s = lax.dot_general(
            kv[:, k * HD : (k + 1) * HD],
            q_all[k, c * width : (c + 1) * width, :],
            (((1,), (1,)), ((), ())),
            preferred_element_type=jnp.float32,
        )
        s = jnp.where(live, s * scale, LOW)
        m = jnp.max(s, 0, keepdims=True)
        return jnp.where(live, jnp.exp(s - m), 0.0), m

    for k in range(heads):
        for c in range(chunks):
            at = slice(c * width, (c + 1) * width)
            e, m = scored(k, c)
            if store:
                e_all[k * chunks + c] = e
            stat[k : k + 1, at] = m
            stat[heads + k : heads + k + 1, at] = jnp.sum(e, 0, keepdims=True)

    def st(i):
        return remote(stat, statr.at[i], st_send.at[i], st_recv.at[i], tp=(me + i) % n)

    every(st, go)
    every(st, got)
    statr[0] = stat[...]

    def top_of(i, running):
        return jnp.maximum(running, statr[i, :heads, :])

    top = lax.fori_loop(1, n, top_of, stat[:heads, :])

    def sum_of(i, running):
        return running + statr[i, heads : 2 * heads, :] * jnp.exp(statr[i, :heads, :] - top)

    sums = lax.fori_loop(0, n, sum_of, jnp.zeros_like(top))
    factor = jnp.exp(stat[:heads, :] - top) / sums

    def mx(k):
        at = pl.ds(k * groups * HD, groups * HD)

        def copy(i):
            j = (me + i) % n
            src = mixed.at[pl.ds(pl.multiple_of(j * both, both), both), at]
            return remote(src, mixr.at[i, :, at], mx_send.at[k, i], mx_recv.at[k, i], tp=j)

        return copy

    for k in range(heads):
        for c in range(chunks):
            e = e_all[k * chunks + c] if store else scored(k, c)[0]
            weights = (e * factor[k : k + 1, c * width : (c + 1) * width]).astype(jnp.bfloat16)
            out = lax.dot_general(
                weights,
                kv[:, half + k * HD : half + (k + 1) * HD],
                (((0,), (0,)), ((), ())),
                preferred_element_type=jnp.float32,
            )
            size = min(width, R)
            for piece in range(width // size):
                head, first = divmod(c * width + piece * size, R)
                at = (k * groups + head) * HD
                mixed[first : first + size, at : at + HD] = out[
                    piece * size : (piece + 1) * size
                ]
        every(mx(k), go)

    for k in range(heads):
        every(mx(k), got)
    attended = total(mixed, mixr)
    att[p, me] = jnp.concatenate([attended[:, : qcols // 2], attended[:, qcols // 2 :]], 0).astype(
        jnp.bfloat16
    )

    def at_copy(c):
        def copy(i):
            q = (p + c) % 2
            return remote(
                att.at[p, me], att.at[p, me], at_send.at[c, i], at_recv.at[c, i], tp=(me + i) % n, pd=q
            )

        return copy

    def at_wait(c):
        def wait(i):
            q = (p + c) % 2
            j = (me + n - i) % n
            remote(
                att.at[q, j], att.at[q, j], at_send.at[c, i], at_recv.at[c, i], tp=j, pd=q
            ).wait_recv()

        return wait

    pl.loop(1, n)(lambda i: go(at_copy(0)(i)))
    pl.loop(0, n)(lambda i: go(at_copy(1)(i)))
    locals_[4].wait()
    pl.loop(1, n)(at_wait(0))
    pl.loop(0, n)(at_wait(1))

    hidden = emb[...]
    for q in range(2):
        got_att = att[q].astype(jnp.float32)
        for h in range(2):
            lhs = got_att[:, h * both : (h + 1) * both, :].reshape(R, qcols // 2)
            at = q * qcols + h * (qcols // 2)
            hidden = hidden + jnp.dot(
                lhs.astype(jnp.bfloat16),
                wo[at : at + qcols // 2, :],
                preferred_element_type=jnp.float32,
            )
    part[...] = jnp.broadcast_to(jnp.sum(hidden * hidden, 1, keepdims=True), (R, 128))
    part[:, :levels] = lax.dot_general(
        hidden * out_gain_ref[...].reshape(1, rows),
        head_ref[...],
        (((1,), (1,)), ((), ())),
        precision=lax.Precision.HIGHEST,
        preferred_element_type=jnp.float32,
    )
    lg = scatter(part, partr, lg_send, lg_recv)
    every(lg, go)
    every(lg, got)
    final = total(part, partr)
    final = final[:, :levels] * lax.rsqrt(final[:, 127:128] / depth + eps)
    out_ref[...] = jnp.where(p == 0, final[:per], final[per:])

    for copy in (rs, ag, st, lg, at_copy(0), *[mx(k) for k in range(heads)]):
        every(copy, sent)
    pl.loop(0, n)(lambda i: sent(at_copy(1)(i)))

    @pl.loop(0, n - 1)
    def _(s):
        for h in range(len(p_parts)):
            p_copy(s, h).wait_send()
        for h in range(len(c_parts)):
            c_copy(s, h).wait_send()

    @pl.loop(1, n)
    def _(s):
        for h in range(len(p_parts)):
            y_copy(s, h).wait_send()


def body(
    prompt_hidden,
    w_kv,
    w_query,
    w_out,
    code_table,
    attn_gain,
    out_gain,
    head_weight,
    decode_codes,
    page_owner,
    page_request,
    page_tokens,
):
    n = lax.axis_size("tp")
    p = lax.axis_index("pd")
    toks, depth = prompt_hidden.shape[2:]
    per = decode_codes.shape[2]
    both = 2 * per
    R = n * both
    rows, kv_width = w_kv.shape
    half = kv_width // 4
    qcols = w_query.shape[1] // 2
    cols = qcols + 2 * half
    heads = half // HD
    groups = qcols // half
    R4 = R * groups
    width = min(256, R4)
    T = 2 * toks + R
    starts = jnp.array([sum(fsq_levels[:d]) for d in range(6)], jnp.int32)
    codes = decode_codes[:, 0].transpose(2, 1, 0).reshape(6, n * per) + starts[:, None]
    target = page_owner.reshape(-1) * both + (1 - p) * per + page_request.reshape(-1)
    pages = jnp.stack([target, page_tokens.reshape(-1)])
    lanes = -(-max(codes.shape[1], pages.shape[1]) // 128) * 128
    meta = jnp.concatenate(
        [jnp.pad(x, ((0, 0), (0, lanes - x.shape[1]))) for x in (codes, pages)], 0
    )

    bf, f32 = jnp.bfloat16, jnp.float32
    store = heads * T * R4 * 4 <= 8 << 20
    dma = pltpu.SemaphoreType.DMA
    hbm = pl.BlockSpec(memory_space=pl.ANY)
    vmem = pl.BlockSpec(memory_space=pltpu.VMEM)
    scratch = [
        pltpu.VMEM((2 * toks, depth), bf),
        pltpu.VMEM((depth, 2 * half), bf),
        pltpu.VMEM((2 * toks, 2 * half), f32),
        pltpu.VMEM((T, 2 * half), bf),
        pltpu.VMEM((rows, qcols), bf),
        pltpu.VMEM(w_out.shape, bf),
        pltpu.VMEM(meta.shape, jnp.int32),
        pltpu.VMEM((R, rows), f32),
        pltpu.VMEM((R, cols + 128), f32),
        pltpu.VMEM((n, both, cols + 128), f32),
        pltpu.VMEM((R, cols), f32),
        pltpu.VMEM((heads, R4, HD), bf),
        pltpu.VMEM((heads * R4 // width, T, width), f32) if store else None,
        pltpu.VMEM((8, R4), f32),
        pltpu.VMEM((n, 8, R4), f32),
        pltpu.VMEM((R, qcols), f32),
        pltpu.VMEM((n, both, qcols), f32),
        pltpu.VMEM((2, n, 2 * both, qcols // 2), bf),
        pltpu.VMEM((R, 128), f32),
        pltpu.VMEM((n, both, 128), f32),
        dma((5,)),
        dma((3,)),
        dma((3,)),
    ] + [dma((PIECES, n))] * 6 + [dma((n,))] * 6 + [dma((heads, n))] * 2 + [dma((2, n))] * 2 + [dma((n,))] * 2
    run = functools.partial(kernel, n, per)
    if not store:
        at = 10 + 12
        scratch.pop(12)
        full = run

        def run(*refs):
            return full(*refs[:at], None, *refs[at:])

    logits = pl.pallas_call(
        run,
        out_shape=jax.ShapeDtypeStruct((per, head_weight.shape[1]), f32),
        in_specs=[hbm, hbm, hbm, hbm, vmem, vmem, vmem, vmem, vmem],
        out_specs=vmem,
        scratch_shapes=scratch,
        compiler_params=pltpu.CompilerParams(
            collective_id=0, has_side_effects=True, vmem_limit_bytes=60 << 20
        ),
    )(
        prompt_hidden.reshape(toks, depth),
        w_kv,
        w_query,
        w_out,
        code_table,
        attn_gain,
        out_gain,
        head_weight.T,
        meta,
    )
    return logits.reshape(1, 1, per, -1)


def solution(mesh):
    return jax.shard_map(
        body,
        mesh=mesh,
        in_specs=(
            P(("grp", "tp"), "pd", None, None),
            P("tp", None),
            P("tp", None),
            P(None, "tp"),
            P(None, "tp"),
            P("tp"),
            P("tp"),
            P("tp", None),
            P("grp", "pd", None, None),
            P(("grp", "tp"), "pd", None, None),
            P(("grp", "tp"), "pd", None),
            P(("grp", "tp"), "pd", None),
        ),
        out_specs=P(("grp", "tp"), "pd", None, None),
        check_vma=False,
    )
```
